32 devices in a mesh: wide: 8 (over z, x), gy: 4 (over y, core).
Axes of the slice: x: 2, y: 2, z: 4, core: 2. Of those that a mesh axis runs over, the one named last changes fastest.
Arguments:
- omega: bfloat16 [64, 512, 1024], P(None, 'wide', 'gy'), may hold values from -6 to 6
- coefficients: float32 [4, 512, 1024], P(None, 'wide', 'gy'), may hold values from -0.75 to 3.6, as said below
- obs_rows: bfloat16 [64, 102400], P(None, ('wide', 'gy')), may hold values from -6 to 6
- obs_cell: int32 [102400], P(('wide', 'gy')), may hold values from 0 to 16383
- obs_count: int32 [32, 32], P(('wide', 'gy')), may hold values from 0 to 128, as said below
Outputs:
- applied: bfloat16 [64, 512, 1024], P(None, 'wide', 'gy')
- gram: float32 [64, 64], replicated
- data_field: bfloat16 [64, 512, 1024], P(None, 'wide', 'gy')
The draws below stay inside these ranges and needn't reach their ends.
Inputs may be any that keep to these rules, and one draw needn't show every extreme that they name: `coefficients`: kappa squared lies in [0.05, 3], the row and column conductivities in [0.3, 3.6], the cross conductivity in [-0.75, 0.75]. `obs_count`: each row sums to at most 3200; some entry equals 128 in every draw, and some owner gets 128 rows from every block.
All inputs are finite; a program needn't handle non-finite values.
Results may differ from the reference program's by a relative error of at most 0.0043.
Values may be sent and summed in bfloat16 or wider, within the bound.
A program may use at most 128 MiB of HBM per device.

```python
import jax
import jax.numpy as jnp
from jax import lax

K = 64
CX = 64
CY = 256
CAP = 128
NX = 512
NY = 1024
OBS_DEV = 3200
NOBS = 102400
N_WIDE = 8
N_GY = 4


def row_ramp():
    rows = jnp.arange(NX, dtype=jnp.float32)[:, None] / NX
    return 1.0 + rows


def draw_coefficients(key, part):
    keys = jax.random.split(jax.random.fold_in(key, 11), 4)
    ramp = row_ramp()
    shape = (NX, NY)
    kappa_sq = jnp.exp(jax.random.uniform(keys[0], shape, jnp.float32, jnp.log(0.05), 0.0)) * ramp
    cond_rows = jax.random.uniform(keys[1], shape, jnp.float32, 0.3, 1.2) * ramp
    cond_cols = jax.random.uniform(keys[2], shape, jnp.float32, 0.3, 1.2) * ramp
    cond_cross = jax.random.uniform(keys[3], shape, jnp.float32, -0.25, 0.25) * ramp
    return jnp.stack([kappa_sq, cond_rows, cond_cols, cond_cross]).astype(jnp.float32)


def draw_omega(key, part):
    keys = jax.random.split(jax.random.fold_in(key, 23), 1)
    values = jnp.clip(jax.random.normal(keys[0], (K, NX, NY), jnp.float32), -6.0, 6.0)
    return values.astype(jnp.bfloat16)


def draw_obs_count(key, part):
    devices_all = N_WIDE * N_GY
    keys = jax.random.split(jax.random.fold_in(key, 37), 2)
    hot_owner = jax.random.randint(keys[0], (), 0, devices_all)
    base = jax.random.randint(keys[1], (devices_all, devices_all), CAP // 4, 3 * CAP // 4)
    column = jnp.arange(devices_all)[None, :] == hot_owner
    return jnp.where(column, CAP, base).astype(jnp.int32)


def set_ends(entries, stream_key, low, high):
    longest = entries.shape.index(max(entries.shape))
    spots = []
    for shift in (0, 1):
        where = [jax.random.randint(jax.random.fold_in(stream_key, axis), (), 0, length) for axis, length in enumerate(entries.shape)]
        where[longest] = (where[longest] + shift) % entries.shape[longest]
        spots.append(tuple(where))
    return entries.at[spots[0]].set(low).at[spots[1]].set(high)


def steps_of(rng, extent, cuts, least, top_value):
    level = 1.0
    for axis_at, shards_of in cuts:
        steps = jax.random.uniform(jax.random.fold_in(jax.random.fold_in(rng, 6), axis_at), (shards_of,), jnp.float32, least / len(cuts), top_value / len(cuts))
        level = level * jnp.repeat(jnp.exp(steps), extent[axis_at] // shards_of).reshape((-1,) + (1,) * (len(extent) - 1 - axis_at))
    return level


def gaussian(rng, dims, deviation, bound, cuts=(), kind=jnp.bfloat16):
    entries = jax.random.normal(rng, dims, jnp.float32) * deviation
    if len(cuts) > 0:
        entries = steps_of(rng, dims, cuts, -0.22, 0.18) * entries
    return jnp.clip(entries, min=-bound, max=bound).astype(kind)


def setup_inputs(seed: int = 0) -> dict:
    key_of = jax.random.split(jax.random.key(seed), 6)
    omega = draw_omega(jax.random.fold_in(key_of[5], 71), 0)
    coefficients = draw_coefficients(jax.random.fold_in(key_of[5], 71), 0)
    obs_rows = gaussian(key_of[2], (K, NOBS), 1.0, 6.0, ((1, 32),))
    obs_cell = set_ends(jax.random.randint(key_of[3], (NOBS,), 0, CX * CY), jax.random.fold_in(key_of[3], 1), 0, (CX * CY) - 1).astype(jnp.int32)
    obs_count = draw_obs_count(jax.random.fold_in(key_of[5], 71), 0)
    return {"omega": omega, "coefficients": coefficients, "obs_rows": obs_rows, "obs_cell": obs_cell, "obs_count": obs_count}


def operator_apply(field, coef):
    kappa_sq = coef[0]
    cond_rows = coef[1]
    cond_cols = coef[2]
    cond_cross = coef[3]
    centre = field[..., 1:-1, 1:-1]
    face_south = 0.5 * (cond_rows[1:-1, 1:-1] + cond_rows[2:, 1:-1])
    face_north = 0.5 * (cond_rows[1:-1, 1:-1] + cond_rows[:-2, 1:-1])
    face_east = 0.5 * (cond_cols[1:-1, 1:-1] + cond_cols[1:-1, 2:])
    face_west = 0.5 * (cond_cols[1:-1, 1:-1] + cond_cols[1:-1, :-2])
    diffusion = face_south * (field[..., 2:, 1:-1] - centre) - face_north * (centre - field[..., :-2, 1:-1])
    diffusion = diffusion + face_east * (field[..., 1:-1, 2:] - centre) - face_west * (centre - field[..., 1:-1, :-2])
    mixed = cond_cross[2:, 1:-1] * (field[..., 2:, 2:] - field[..., 2:, :-2]) - cond_cross[:-2, 1:-1] * (field[..., :-2, 2:] - field[..., :-2, :-2])
    mixed = mixed + cond_cross[1:-1, 2:] * (field[..., 2:, 2:] - field[..., :-2, 2:]) - cond_cross[1:-1, :-2] * (field[..., 2:, :-2] - field[..., :-2, :-2])
    return kappa_sq[1:-1, 1:-1] * centre - diffusion - 0.25 * mixed


def reference(omega, coefficients, obs_rows, obs_cell, obs_count):
    coef_pad = jnp.pad(coefficients, ((0, 0), (1, 1), (1, 1)))

    def one_column(column):
        padded = jnp.pad(column.astype(jnp.float32), 1)
        image = operator_apply(padded, coef_pad).astype(jnp.bfloat16)
        image = lax.optimization_barrier(image)
        second = operator_apply(jnp.pad(image.astype(jnp.float32), 1), coef_pad)
        return (0.0625 * second).astype(jnp.bfloat16)

    applied = lax.map(one_column, omega)

    flat_omega = omega.reshape(K, NX * NY)
    flat_applied = applied.reshape(K, NX * NY)
    block_len = CX * NY

    def add_block(index, total):
        start = (index * block_len).astype(jnp.int32)
        left = lax.dynamic_slice_in_dim(flat_omega, start, block_len, 1)
        right = lax.dynamic_slice_in_dim(flat_applied, start, block_len, 1)
        return total + jnp.dot(left, right.T, preferred_element_type=jnp.float32)

    gram = lax.fori_loop(0, N_WIDE, add_block, jnp.zeros((K, K), jnp.float32)) / (NX * NY)

    devices_all = N_WIDE * N_GY

    def cells_of(args):
        counts_row, cells_row = args
        ends = jnp.cumsum(counts_row).astype(jnp.int32)
        position = jnp.arange(OBS_DEV, dtype=jnp.int32)
        owner = jnp.sum((position[:, None] >= ends[None, :]).astype(jnp.int32), axis=1).astype(jnp.int32)
        owner = jnp.minimum(owner, devices_all - 1)
        used = position < ends[devices_all - 1]
        grid_row = (owner // N_GY) * CX + cells_row // CY
        grid_col = (owner % N_GY) * CY + cells_row % CY
        return jnp.where(used, grid_row * NY + grid_col, NX * NY).astype(jnp.int32)

    flat_cells = lax.map(cells_of, (obs_count, obs_cell.reshape(devices_all, OBS_DEV))).reshape(NOBS)

    def bin_column(values):
        binned = jnp.zeros((NX * NY,), jnp.float32).at[flat_cells].add(values.astype(jnp.float32), mode="drop")
        return binned.astype(jnp.bfloat16)

    data_field = lax.map(bin_column, obs_rows).reshape(K, NX, NY)
    return applied, gram, data_field
```

```python
import jax
import jax.numpy as jnp
from jax import lax
from jax.experimental import pallas as pl
from jax.experimental.pallas import tpu as pltpu
from jax.sharding import PartitionSpec as P

CAP = 128


def with_halo(block, sides, width):
    for axis, dim in sides:
        count = lax.axis_size(axis)
        forward = [(i, i + 1) for i in range(count - 1)]
        backward = [(target, source) for source, target in forward]
        low = lax.ppermute(
            lax.slice_in_dim(block, block.shape[dim] - width, None, axis=dim), axis, forward
        )
        high = lax.ppermute(lax.slice_in_dim(block, 0, width, axis=dim), axis, backward)
        block = jnp.concatenate([low, block, high], axis=dim)
    return block


def operator_apply(field, coef):
    kappa_sq = coef[0]
    cond_rows = coef[1]
    cond_cols = coef[2]
    cond_cross = coef[3]
    centre = field[..., 1:-1, 1:-1]
    face_south = 0.5 * (cond_rows[1:-1, 1:-1] + cond_rows[2:, 1:-1])
    face_north = 0.5 * (cond_rows[1:-1, 1:-1] + cond_rows[:-2, 1:-1])
    face_east = 0.5 * (cond_cols[1:-1, 1:-1] + cond_cols[1:-1, 2:])
    face_west = 0.5 * (cond_cols[1:-1, 1:-1] + cond_cols[1:-1, :-2])
    diffusion = face_south * (field[..., 2:, 1:-1] - centre) - face_north * (
        centre - field[..., :-2, 1:-1]
    )
    diffusion = (
        diffusion
        + face_east * (field[..., 1:-1, 2:] - centre)
        - face_west * (centre - field[..., 1:-1, :-2])
    )
    mixed = cond_cross[2:, 1:-1] * (field[..., 2:, 2:] - field[..., 2:, :-2]) - cond_cross[
        :-2, 1:-1
    ] * (field[..., :-2, 2:] - field[..., :-2, :-2])
    mixed = (
        mixed
        + cond_cross[1:-1, 2:] * (field[..., 2:, 2:] - field[..., :-2, 2:])
        - cond_cross[1:-1, :-2] * (field[..., 2:, :-2] - field[..., :-2, :-2])
    )
    return kappa_sq[1:-1, 1:-1] * centre - diffusion - 0.25 * mixed


def pack_kernel(counts_ref, rows_ref, cells_ref, out_ref):
    owners, _, _ = out_ref.shape
    columns, length = rows_ref.shape
    window = 2 * CAP
    tile_cols = 256
    slot = lax.broadcasted_iota(jnp.int32, (1, CAP), 1)
    sub = lax.broadcasted_iota(jnp.int32, (16, CAP), 0)

    def body(o, start):
        count = counts_ref[o]
        base = jnp.minimum((start // CAP) * CAP, length - window)
        base = pl.multiple_of(base, CAP)
        shift = lax.rem(2 * window - (start - base), window)
        rows = rows_ref[:, pl.ds(base, window)].astype(jnp.float32)
        rows = pltpu.roll(rows, shift, 1)[:, :CAP]
        used = slot < count
        out_ref[o, 0:columns, :] = jnp.where(used, rows, 0.0).astype(jnp.bfloat16)
        cells = jnp.broadcast_to(cells_ref[:, pl.ds(base, window)], (8, window))
        cells = pltpu.roll(cells, shift, 1)[0:1, :CAP]
        cell_row = jnp.where(used, cells // tile_cols, 128)
        cell_col = jnp.where(used, cells % tile_cols, 0)
        both = jnp.where(sub == 0, cell_row, jnp.where(sub == 1, cell_col, 0))
        out_ref[o, columns : columns + 16, :] = both.astype(jnp.float32).astype(jnp.bfloat16)
        return start + count

    lax.fori_loop(0, owners, body, jnp.int32(0))


def pack_windows(counts, rows, cells):
    columns = rows.shape[0]
    owners = counts.shape[0]
    smem = pl.BlockSpec(memory_space=pltpu.SMEM)
    vmem = pl.BlockSpec(memory_space=pltpu.VMEM)
    return pl.pallas_call(
        pack_kernel,
        out_shape=jax.ShapeDtypeStruct((owners, columns + 16, CAP), jnp.bfloat16),
        in_specs=[smem, vmem, vmem],
        out_specs=vmem,
        compiler_params=pltpu.CompilerParams(vmem_limit_bytes=40 * 1024 * 1024),
    )(counts, rows, cells.reshape(1, -1))


GROUP = 8
SLOTS = 1024


def bin_kernel(got_ref, out_ref, rows_all, row_hot, col_hot, lhs, total):
    sources, wide_rows, _ = got_ref.shape
    columns = wide_rows - 16
    _, tile_rows, tile_cols = out_ref.shape
    step = pl.program_id(0)

    @pl.when(step == 0)
    def _():
        row_id = lax.broadcasted_iota(jnp.int32, (tile_rows, CAP), 0)
        col_id = lax.broadcasted_iota(jnp.int32, (tile_cols, CAP), 0)

        def body(d, carry):
            at = pl.ds(pl.multiple_of(d * CAP, CAP), CAP)
            rows_all[:, at] = got_ref[d, 0:columns, :].astype(jnp.float32)
            cells = got_ref[d, columns : columns + 16, :].astype(jnp.float32).astype(jnp.int32)
            hot = jnp.where(row_id == cells[0:1, :], 1.0, 0.0)
            row_hot[:, at] = hot.astype(jnp.bfloat16)
            hot = jnp.where(col_id == cells[1:2, :], 1.0, 0.0)
            col_hot[at, :] = hot.T.astype(jnp.bfloat16)
            return carry

        lax.fori_loop(0, sources, body, 0)

    total[...] = jnp.zeros_like(total)
    group_at = pl.ds(pl.multiple_of(step * GROUP, GROUP), GROUP)

    def chunk(c, carry):
        at = pl.ds(pl.multiple_of(c * SLOTS, SLOTS), SLOTS)
        values = rows_all[group_at, at]
        mask = row_hot[:, at]
        for i in range(GROUP):
            row = jnp.broadcast_to(values[i : i + 1, :], (tile_rows, SLOTS)).astype(jnp.bfloat16)
            lhs[i * tile_rows : (i + 1) * tile_rows, :] = row * mask
        total[...] += jnp.dot(lhs[...], col_hot[at, :], preferred_element_type=jnp.float32)
        return carry

    lax.fori_loop(0, (sources * CAP) // SLOTS, chunk, 0)
    out_ref[...] = total[...].reshape(GROUP, tile_rows, tile_cols).astype(jnp.bfloat16)


def bin_rows(got, columns, tile_rows, tile_cols):
    slots = got.shape[0] * CAP
    return pl.pallas_call(
        bin_kernel,
        grid=(columns // GROUP,),
        out_shape=jax.ShapeDtypeStruct((columns, tile_rows, tile_cols), jnp.bfloat16),
        in_specs=[pl.BlockSpec(got.shape, lambda i: (0, 0, 0))],
        out_specs=pl.BlockSpec((GROUP, tile_rows, tile_cols), lambda i: (i, 0, 0)),
        scratch_shapes=[
            pltpu.VMEM((columns, slots), jnp.float32),
            pltpu.VMEM((tile_rows, slots), jnp.bfloat16),
            pltpu.VMEM((slots, tile_cols), jnp.bfloat16),
            pltpu.VMEM((GROUP * tile_rows, SLOTS), jnp.bfloat16),
            pltpu.VMEM((GROUP * tile_rows, tile_cols), jnp.float32),
        ],
        compiler_params=pltpu.CompilerParams(vmem_limit_bytes=40 * 1024 * 1024),
    )(got)


def per_device(omega, coefficients, obs_rows, obs_cell, obs_count):
    columns, tile_rows, tile_cols = omega.shape
    wide_count = lax.axis_size("wide")
    gy_count = lax.axis_size("gy")
    devices_all = wide_count * gy_count
    coef_pad = with_halo(coefficients, (("wide", 1), ("gy", 2)), 1)
    sketch_pad = with_halo(omega, (("wide", 1), ("gy", 2)), 1)
    image = operator_apply(sketch_pad.astype(jnp.float32), coef_pad).astype(jnp.bfloat16)
    image = lax.optimization_barrier(image)
    image_pad = with_halo(image, (("wide", 1), ("gy", 2)), 1)
    second = operator_apply(image_pad.astype(jnp.float32), coef_pad)
    applied = (0.0625 * second).astype(jnp.bfloat16)
    local_gram = lax.dot_general(
        omega.reshape(columns, tile_rows * tile_cols),
        applied.reshape(columns, tile_rows * tile_cols),
        (((1,), (1,)), ((), ())),
        preferred_element_type=jnp.float32,
    )
    copies = jnp.broadcast_to(local_gram[None], (devices_all,) + local_gram.shape)
    terms = lax.all_to_all(copies, ("wide", "gy"), split_axis=0, concat_axis=0, tiled=True)
    summed = jnp.sum(terms, axis=0)
    gram = summed / (tile_rows * tile_cols * devices_all)
    counts_row = obs_count[0]
    packed = pack_windows(counts_row, obs_rows, obs_cell)
    got = lax.all_to_all(packed, ("wide", "gy"), split_axis=0, concat_axis=0, tiled=True)
    data_field = bin_rows(got, columns, tile_rows, tile_cols)
    return (applied, gram, data_field)


def solution(mesh):
    in_specs = (
        P(None, "wide", "gy"),
        P(None, "wide", "gy"),
        P(None, ("wide", "gy")),
        P(("wide", "gy")),
        P(("wide", "gy"), None),
    )
    out_specs = (P(None, "wide", "gy"), P(), P(None, "wide", "gy"))
    return jax.shard_map(
        per_device, mesh=mesh, in_specs=in_specs, out_specs=out_specs, check_vma=False
    )
```

```python
import functools

import jax
import jax.numpy as jnp
from jax import lax
from jax.experimental import pallas as pl
from jax.experimental.pallas import tpu as pltpu
from jax.sharding import PartitionSpec as P

CAP = 128


def with_halo(block, sides, width):
    for axis, dim in sides:
        count = lax.axis_size(axis)
        forward = [(i, i + 1) for i in range(count - 1)]
        backward = [(target, source) for source, target in forward]
        low = lax.ppermute(
            lax.slice_in_dim(block, block.shape[dim] - width, None, axis=dim), axis, forward
        )
        high = lax.ppermute(lax.slice_in_dim(block, 0, width, axis=dim), axis, backward)
        block = jnp.concatenate([low, block, high], axis=dim)
    return block


def halo_of(block, sides):
    parts = []
    for axis, dim in sides:
        count = lax.axis_size(axis)
        forward = [(i, i + 1) for i in range(count - 1)]
        backward = [(target, source) for source, target in forward]
        first = lax.slice_in_dim(block, 0, 1, axis=dim)
        last = lax.slice_in_dim(block, block.shape[dim] - 1, None, axis=dim)
        if parts:
            north, south = parts
            cut = lambda a, at: lax.slice_in_dim(a, at, at + 1, axis=dim)
            end = block.shape[dim] - 1
            first = jnp.concatenate([cut(north, 0), first, cut(south, 0)], axis=dim - 1)
            last = jnp.concatenate([cut(north, end), last, cut(south, end)], axis=dim - 1)
        low = lax.ppermute(last, axis, forward)
        high = lax.ppermute(first, axis, backward)
        parts = parts + [low, high]
    return parts


def stencil_planes(coef):
    def face(c, di, dj):
        near = c[1 + di : c.shape[0] - 1 + di, 1 + dj : c.shape[1] - 1 + dj]
        return near

    rows, cols, cross = coef[1], coef[2], coef[3]
    south = 0.5 * (face(rows, 0, 0) + face(rows, 1, 0))
    north = 0.5 * (face(rows, 0, 0) + face(rows, -1, 0))
    east = 0.5 * (face(cols, 0, 0) + face(cols, 0, 1))
    west = 0.5 * (face(cols, 0, 0) + face(cols, 0, -1))
    cs, cn = 0.25 * face(cross, 1, 0), 0.25 * face(cross, -1, 0)
    ce, cw = 0.25 * face(cross, 0, 1), 0.25 * face(cross, 0, -1)
    centre = face(coef[0], 0, 0) + south + north + east + west
    return jnp.stack(
        [-(cn + cw), -north, cn + ce, -west, centre, -east, cs + cw, -south, -(cs + ce)]
    )


def stencil_kernel(scale, planes, field, north, south, west, east, out):
    group, tile_rows, tile_cols = field.shape
    row = lax.broadcasted_iota(jnp.int32, (tile_rows, tile_cols), 0)
    col = lax.broadcasted_iota(jnp.int32, (tile_rows, tile_cols), 1)
    for k in range(group):
        v = field[k].astype(jnp.float32)
        top = north[k].astype(jnp.float32)
        bottom = south[k].astype(jnp.float32)
        low = west[k].astype(jnp.float32)
        high = east[k].astype(jnp.float32)
        up = jnp.where(row == 0, top, pltpu.roll(v, 1, 0))
        down = jnp.where(row == tile_rows - 1, bottom, pltpu.roll(v, tile_rows - 1, 0))
        total = None
        for i, line in enumerate((up, v, down)):
            left = jnp.where(col == 0, low[i : i + tile_rows], pltpu.roll(line, 1, 1))
            right = jnp.where(
                col == tile_cols - 1,
                high[i : i + tile_rows],
                pltpu.roll(line, tile_cols - 1, 1),
            )
            term = planes[3 * i] * left + planes[3 * i + 1] * line + planes[3 * i + 2] * right
            total = term if total is None else total + term
        out[k] = (scale * total).astype(jnp.bfloat16)


def stencil(field, planes, scale):
    columns, tile_rows, tile_cols = field.shape
    sides = halo_of(field, (("wide", 1), ("gy", 2)))
    group = 8
    by_column = lambda a: pl.BlockSpec((group,) + a.shape[1:], lambda i: (i, 0, 0))
    return pl.pallas_call(
        functools.partial(stencil_kernel, scale),
        grid=(columns // group,),
        out_shape=jax.ShapeDtypeStruct(field.shape, jnp.bfloat16),
        in_specs=[pl.BlockSpec(planes.shape, lambda i: (0, 0, 0)), by_column(field)]
        + [by_column(a) for a in sides],
        out_specs=by_column(field),
        compiler_params=pltpu.CompilerParams(vmem_limit_bytes=40 * 1024 * 1024),
    )(planes, field, *sides)


def pack_kernel(counts_ref, rows_ref, cells_ref, out_ref):
    owners, _, _ = out_ref.shape
    columns, length = rows_ref.shape
    window = 2 * CAP
    tile_cols = 256
    slot = lax.broadcasted_iota(jnp.int32, (1, CAP), 1)
    sub = lax.broadcasted_iota(jnp.int32, (16, CAP), 0)

    def body(o, start):
        count = counts_ref[o]
        base = jnp.minimum((start // CAP) * CAP, length - window)
        base = pl.multiple_of(base, CAP)
        shift = lax.rem(2 * window - (start - base), window)
        rows = rows_ref[:, pl.ds(base, window)].astype(jnp.float32)
        rows = pltpu.roll(rows, shift, 1)[:, :CAP]
        used = slot < count
        out_ref[o, 0:columns, :] = jnp.where(used, rows, 0.0).astype(jnp.bfloat16)
        cells = jnp.broadcast_to(cells_ref[:, pl.ds(base, window)], (8, window))
        cells = pltpu.roll(cells, shift, 1)[0:1, :CAP]
        cell_row = jnp.where(used, cells // tile_cols, 128)
        cell_col = jnp.where(used, cells % tile_cols, 0)
        both = jnp.where(sub == 0, cell_row, jnp.where(sub == 1, cell_col, 0))
        out_ref[o, columns : columns + 16, :] = both.astype(jnp.float32).astype(jnp.bfloat16)
        return start + count

    lax.fori_loop(0, owners, body, jnp.int32(0))


def pack_windows(counts, rows, cells):
    columns = rows.shape[0]
    owners = counts.shape[0]
    smem = pl.BlockSpec(memory_space=pltpu.SMEM)
    vmem = pl.BlockSpec(memory_space=pltpu.VMEM)
    return pl.pallas_call(
        pack_kernel,
        out_shape=jax.ShapeDtypeStruct((owners, columns + 16, CAP), jnp.bfloat16),
        in_specs=[smem, vmem, vmem],
        out_specs=vmem,
        compiler_params=pltpu.CompilerParams(vmem_limit_bytes=40 * 1024 * 1024),
    )(counts, rows, cells.reshape(1, -1))


GROUP = 8
SLOTS = 1024


def bin_kernel(got_ref, out_ref, rows_all, row_hot, col_hot, lhs, total):
    sources, wide_rows, _ = got_ref.shape
    columns = wide_rows - 16
    _, tile_rows, tile_cols = out_ref.shape
    step = pl.program_id(0)

    @pl.when(step == 0)
    def _():
        row_id = lax.broadcasted_iota(jnp.int32, (tile_rows, CAP), 0)
        col_id = lax.broadcasted_iota(jnp.int32, (tile_cols, CAP), 0)

        def body(d, carry):
            at = pl.ds(pl.multiple_of(d * CAP, CAP), CAP)
            rows_all[:, at] = got_ref[d, 0:columns, :].astype(jnp.float32)
            cells = got_ref[d, columns : columns + 16, :].astype(jnp.float32).astype(jnp.int32)
            hot = jnp.where(row_id == cells[0:1, :], 1.0, 0.0)
            row_hot[:, at] = hot.astype(jnp.bfloat16)
            hot = jnp.where(col_id == cells[1:2, :], 1.0, 0.0)
            col_hot[at, :] = hot.T.astype(jnp.bfloat16)
            return carry

        lax.fori_loop(0, sources, body, 0)

    total[...] = jnp.zeros_like(total)
    group_at = pl.ds(pl.multiple_of(step * GROUP, GROUP), GROUP)

    def chunk(c, carry):
        at = pl.ds(pl.multiple_of(c * SLOTS, SLOTS), SLOTS)
        values = rows_all[group_at, at]
        mask = row_hot[:, at]
        for i in range(GROUP):
            row = jnp.broadcast_to(values[i : i + 1, :], (tile_rows, SLOTS)).astype(jnp.bfloat16)
            lhs[i * tile_rows : (i + 1) * tile_rows, :] = row * mask
        total[...] += jnp.dot(lhs[...], col_hot[at, :], preferred_element_type=jnp.float32)
        return carry

    lax.fori_loop(0, (sources * CAP) // SLOTS, chunk, 0)
    out_ref[...] = total[...].reshape(GROUP, tile_rows, tile_cols).astype(jnp.bfloat16)


def bin_rows(got, columns, tile_rows, tile_cols):
    slots = got.shape[0] * CAP
    return pl.pallas_call(
        bin_kernel,
        grid=(columns // GROUP,),
        out_shape=jax.ShapeDtypeStruct((columns, tile_rows, tile_cols), jnp.bfloat16),
        in_specs=[pl.BlockSpec(got.shape, lambda i: (0, 0, 0))],
        out_specs=pl.BlockSpec((GROUP, tile_rows, tile_cols), lambda i: (i, 0, 0)),
        scratch_shapes=[
            pltpu.VMEM((columns, slots), jnp.float32),
            pltpu.VMEM((tile_rows, slots), jnp.bfloat16),
            pltpu.VMEM((slots, tile_cols), jnp.bfloat16),
            pltpu.VMEM((GROUP * tile_rows, SLOTS), jnp.bfloat16),
            pltpu.VMEM((GROUP * tile_rows, tile_cols), jnp.float32),
        ],
        compiler_params=pltpu.CompilerParams(vmem_limit_bytes=40 * 1024 * 1024),
    )(got)


def per_device(omega, coefficients, obs_rows, obs_cell, obs_count):
    columns, tile_rows, tile_cols = omega.shape
    wide_count = lax.axis_size("wide")
    gy_count = lax.axis_size("gy")
    devices_all = wide_count * gy_count
    coef_pad = with_halo(coefficients, (("wide", 1), ("gy", 2)), 1)
    planes = stencil_planes(coef_pad)
    image = stencil(omega, planes, 1.0)
    applied = stencil(image, planes, 0.0625)
    local_gram = lax.dot_general(
        omega.reshape(columns, tile_rows * tile_cols),
        applied.reshape(columns, tile_rows * tile_cols),
        (((1,), (1,)), ((), ())),
        preferred_element_type=jnp.float32,
    )
    copies = jnp.broadcast_to(local_gram[None], (devices_all,) + local_gram.shape)
    terms = lax.all_to_all(copies, ("wide", "gy"), split_axis=0, concat_axis=0, tiled=True)
    summed = jnp.sum(terms, axis=0)
    gram = summed / (tile_rows * tile_cols * devices_all)
    counts_row = obs_count[0]
    packed = pack_windows(counts_row, obs_rows, obs_cell)
    got = lax.all_to_all(packed, ("wide", "gy"), split_axis=0, concat_axis=0, tiled=True)
    data_field = bin_rows(got, columns, tile_rows, tile_cols)
    return (applied, gram, data_field)


def solution(mesh):
    in_specs = (
        P(None, "wide", "gy"),
        P(None, "wide", "gy"),
        P(None, ("wide", "gy")),
        P(("wide", "gy")),
        P(("wide", "gy"), None),
    )
    out_specs = (P(None, "wide", "gy"), P(), P(None, "wide", "gy"))
    return jax.shard_map(
        per_device, mesh=mesh, in_specs=in_specs, out_specs=out_specs, check_vma=False
    )
```
